32 devices in a mesh: row: 2 (over y), col: 16 (over z, x, core).
Axes of the slice: x: 2, y: 2, z: 4, core: 2. Of those that a mesh axis runs over, the one named last changes fastest.
Arguments:
- inputs: bfloat16 [512, 9216], P('col', 'row'), may hold values from -6 to 6
- out_grad: bfloat16 [512, 9216], P('col', 'row'), may hold values from -6 to 6
- preact: bfloat16 [512, 36864], P('row', 'col'), may hold values from -6 to 6
- first_weight: bfloat16 [9216, 36864], P('row', 'col'), may hold values from -0.0625 to 0.0625
- second_weight: bfloat16 [36864, 9216], P('col', 'row'), may hold values from -0.03125 to 0.03125
Outputs:
- grad_inputs: float32 [512, 9216], P('col', 'row')
- grad_first: bfloat16 [9216, 36864], P('row', 'col')
- grad_second: bfloat16 [36864, 9216], P('col', 'row')
The draws below stay inside these ranges and needn't reach their ends.
All inputs are finite; a program needn't handle non-finite values.
Results may differ from the reference program's by a relative error of at most 0.005.
Values may be sent and summed in bfloat16 or wider, within the bound.
A program may use at most 192 MiB of HBM per device.

```python
import math
import jax
import jax.numpy as jnp
from jax import lax

D = 9216
FF = 36864
TOKENS = 512


def block_levels(stream_key, shape, pieces, least, high):
    def one(dim, parts):
        heights = jax.random.uniform(jax.random.fold_in(jax.random.fold_in(stream_key, 6), dim), (parts,), jnp.float32, least / len(pieces), high / len(pieces))
        return jnp.repeat(jnp.exp(heights), shape[dim] // parts).reshape((-1,) + (1,) * (len(shape) - dim - 1))

    factor_of = one(*pieces[0])
    for cut in pieces[1:]:
        factor_of = factor_of * one(*cut)
    return factor_of


def normal_values(key, shape, width, reach, pieces=(), kind=jnp.bfloat16):
    values = jax.random.normal(key, shape, jnp.float32) * width
    if len(pieces) > 0:
        values = block_levels(key, shape, pieces, -0.22, 0.18) * values
    return jnp.clip(values, min=-reach, max=reach).astype(kind)


def setup_inputs(seed: int = 0) -> dict:
    keys = jax.random.split(jax.random.key(seed), 6)
    return {
        "inputs": normal_values(keys[0], (TOKENS, D), 1.0, 6.0, ((0, 16), (1, 2))),
        "out_grad": normal_values(keys[1], (TOKENS, D), 1.0, 6.0, ((0, 16), (1, 2))),
        "preact": normal_values(keys[2], (TOKENS, FF), 1.0, 6.0, ((0, 2), (1, 16))),
        "first_weight": normal_values(keys[3], (D, FF), D ** -0.5, 0.0625, ((0, 2), (1, 16))),
        "second_weight": normal_values(keys[4], (FF, D), FF ** -0.5, 0.03125, ((0, 16), (1, 2))),
    }


INV_ROOT_TWO = 0.7071067811865476
INV_ROOT_TWO_PI = 0.3989422804014327

def gelu_value(values):
    return 0.5 * values * (1.0 + lax.erf(values * INV_ROOT_TWO))

def gelu_slope(values):
    normal_cdf = 0.5 * (1.0 + lax.erf(values * INV_ROOT_TWO))
    density = jnp.exp(-0.5 * values * values) * INV_ROOT_TWO_PI
    return normal_cdf + values * density

def reference(inputs, out_grad, preact, first_weight, second_weight):
    factor = 1.0 / math.sqrt(TOKENS)
    hidden_pre = preact.astype(jnp.float32)
    activated = gelu_value(hidden_pre).astype(jnp.bfloat16)
    slopes = gelu_slope(hidden_pre)
    blocks = math.gcd(FF, 8)
    block_cols = FF // blocks

    def step(grad_total, block_id):
        offset = (block_id * block_cols).astype(jnp.int32)
        first_part = lax.dynamic_slice_in_dim(first_weight, offset, block_cols, 1)
        second_part = lax.dynamic_slice_in_dim(second_weight, offset, block_cols, 0)
        grad_act = lax.dot_general(out_grad, second_part, (((1,), (1,)), ((), ())), preferred_element_type=jnp.float32)
        slope_part = lax.dynamic_slice_in_dim(slopes, offset, block_cols, 1)
        grad_pre = (grad_act * slope_part).astype(jnp.bfloat16)
        act_part = lax.dynamic_slice_in_dim(activated, offset, block_cols, 1)
        first_part_grad = (lax.dot_general(inputs, grad_pre, (((0,), (0,)), ((), ())), preferred_element_type=jnp.float32) * factor).astype(jnp.bfloat16)
        second_part_grad = (lax.dot_general(act_part, out_grad, (((0,), (0,)), ((), ())), preferred_element_type=jnp.float32) * factor).astype(jnp.bfloat16)
        grad_total = grad_total + lax.dot_general(grad_pre, first_part, (((1,), (1,)), ((), ())), preferred_element_type=jnp.float32)
        return (grad_total, (first_part_grad, second_part_grad))
    grad_total, (first_parts, second_parts) = lax.scan(step, jnp.zeros((TOKENS, D), jnp.float32), jnp.arange(blocks, dtype=jnp.int32))
    grad_first = jnp.transpose(first_parts, (1, 0, 2)).reshape(D, FF)
    grad_second = second_parts.reshape(FF, D)
    return (grad_total, grad_first, grad_second)
```

```python
import functools
import math

import jax
import jax.numpy as jnp
from jax import lax
from jax.experimental import pallas as pl
from jax.experimental.pallas import tpu as pltpu
from jax.sharding import PartitionSpec as P

INV_ROOT_TWO = 0.7071067811865476
INV_ROOT_TWO_PI = 0.3989422804014327
MESH = pl.DeviceIdType.MESH
VMEM_LIMIT = 58 * 1024 * 1024


def gelu_value(values):
    return 0.5 * values * (1.0 + lax.erf(values * INV_ROOT_TWO))


def gelu_slope(values):
    normal_cdf = 0.5 * (1.0 + lax.erf(values * INV_ROOT_TWO))
    density = jnp.exp(-0.5 * values * values) * INV_ROOT_TWO_PI
    return normal_cdf + values * density


def contract_rows(left, right):
    return lax.dot_general(
        left, right, (((0,), (0,)), ((), ())), preferred_element_type=jnp.float32
    )


def contract_cols(left, right):
    return lax.dot_general(
        left, right, (((1,), (1,)), ((), ())), preferred_element_type=jnp.float32
    )


def tile_of(size):
    return next(t for t in (256, 384, 128, size) if size % t == 0)


def cut_of(width):
    return width // 256 * 128


def ring_position(chip, chips):
    odd = lax.rem(chip, 2)
    half = lax.div(chip, 2)
    return half + odd * (chips - 1 - 2 * half)


def ring_chip(position, chips):
    evens = (chips + 1) // 2
    position = lax.rem(position + 2 * chips, chips)
    upper = (position >= evens).astype(jnp.int32)
    return 2 * position + upper * (2 * (chips - 1 - position) + 1 - 2 * position)


def enter(col_peers, row_size, row):
    barrier = pltpu.get_barrier_semaphore()
    for peer in col_peers:
        pl.semaphore_signal(barrier, inc=1, device_id={"col": peer}, device_id_type=MESH)
    for shift in range(1, row_size):
        pl.semaphore_signal(
            barrier, inc=1, device_id={"row": lax.rem(row + shift, row_size)}, device_id_type=MESH
        )
    pl.semaphore_wait(barrier, len(col_peers) + row_size - 1)


def gather_kernel(
    row_size, chips, grad_ref, pre_ref, weight_ref,
    full_ref, pre_full_ref, sum_ref, low_ref,
    weight, rows, out_sum, out_low,
    weight_sem, local_sem, side_send, side_recv, pre_send, pre_recv,
    right_send, right_recv, left_send, left_recv, store_sem,
):
    row, col = lax.axis_index("row"), lax.axis_index("col")
    chip, core = lax.div(col, 2), lax.rem(col, 2)
    place = ring_position(chip, chips)
    at = lambda delta: 2 * ring_chip(place + delta, chips) + core
    right, left, side = at(1), at(-1), 2 * chip + 1 - core
    half = chips // 2
    tile = tile_of(weight.shape[0])
    tiles = weight.shape[0] // tile
    block = grad_ref.shape[0]
    width = grad_ref.shape[1]
    cut = cut_of(width)

    def weight_copy(j):
        piece = pl.ds(j * tile, tile)
        return pltpu.make_async_copy(weight_ref.at[piece], weight.at[piece], weight_sem.at[j])

    own = pltpu.make_async_copy(grad_ref, full_ref.at[col], local_sem.at[0])
    own.start()
    for j in range(tiles):
        weight_copy(j).start()
    pre_own = pltpu.make_async_copy(pre_ref, pre_full_ref.at[row], local_sem.at[1])
    pre_own.start()
    enter((right, left, side), row_size, row)
    own.wait()

    def to_col(index, lo, size, peer, send, recv):
        piece = full_ref.at[index, :, pl.ds(lo, size)]
        return pltpu.make_async_remote_copy(
            src_ref=piece, dst_ref=piece, send_sem=send, recv_sem=recv,
            device_id={"col": peer}, device_id_type=MESH,
        )

    def go_right(step):
        size = cut if step == half else width
        return to_col(at(1 - step), 0, size, right, right_send.at[step - 1], right_recv.at[step - 1])

    def go_left(step):
        lo, size = (cut, width - cut) if step == half else (0, width)
        return to_col(at(step - 1), lo, size, left, left_send.at[step - 1], left_recv.at[step - 1])

    def from_left(step):
        size = cut if step == half else width
        return to_col(at(-step), 0, size, right, right_send.at[step - 1], right_recv.at[step - 1])

    def from_right(step):
        lo, size = (cut, width - cut) if step == half else (0, width)
        return to_col(at(step), lo, size, left, left_send.at[step - 1], left_recv.at[step - 1])

    def sideways(delta, mine, slot):
        index = at(delta)
        if not mine:
            index = index + 1 - 2 * core
        return to_col(index, 0, width, side, side_send.at[slot], side_recv.at[slot])

    go_right(1).start()
    go_left(1).start()
    sideways(0, True, 0).start()
    pre_copies = []
    for shift in range(1, row_size):
        pre_copies.append(pltpu.make_async_remote_copy(
            src_ref=pre_ref, dst_ref=pre_full_ref.at[row],
            send_sem=pre_send.at[shift - 1], recv_sem=pre_recv.at[shift - 1],
            device_id={"row": lax.rem(row + shift, row_size)}, device_id_type=MESH,
        ))
        pre_copies[-1].start()

    def multiply(deltas, first):
        count = 2 * block * len(deltas)
        for i, delta in enumerate(deltas):
            origin = 2 * ring_chip(place + delta, chips)
            for k in range(2):
                rows[pl.ds((2 * i + k) * block, block), :] = full_ref[origin + k]

        @pl.loop(0, tiles)
        def _(j):
            piece = pl.ds(pl.multiple_of(j * tile, tile), tile)
            if first:
                pltpu.make_async_copy(
                    weight_ref.at[piece], weight.at[piece], weight_sem.at[j]
                ).wait()
            part = contract_cols(rows[pl.ds(0, count), :], weight[piece, :])
            low = part.astype(jnp.bfloat16)
            for i, delta in enumerate(deltas):
                origin = pl.multiple_of(2 * block * ring_chip(place + delta, chips), 2 * block)
                out_sum[pl.ds(origin, 2 * block), piece] = part[2 * block * i:2 * block * (i + 1)]
                out_low[pl.ds(origin, 2 * block), piece] = low[2 * block * i:2 * block * (i + 1)]

    slot = 1
    sideways(0, False, 0).wait_recv()
    for step in range(1, half + 1):
        deltas = (0,) if step == 1 else (step - 1, 1 - step)
        multiply(deltas, step == 1)
        from_left(step).wait_recv()
        if step < half:
            go_right(step + 1).start()
        from_right(step).wait_recv()
        if step < half:
            go_left(step + 1).start()
        moved = (half,) if step == half else (step, -step)
        for i, delta in enumerate(moved):
            sideways(delta, True, slot + i).start()
        for i, delta in enumerate(moved):
            sideways(delta, False, slot + i).wait_recv()
        slot += len(moved)
    multiply((half,), False)

    out_copies = [
        pltpu.make_async_copy(out_sum, sum_ref, store_sem.at[0]),
        pltpu.make_async_copy(out_low, low_ref, store_sem.at[1]),
    ]
    for copy in out_copies:
        copy.start()
    for step in range(1, half + 1):
        go_right(step).wait_send()
        go_left(step).wait_send()
    slot = 0
    for step in range(0, half + 1):
        moved = (step,) if step in (0, half) else (step, -step)
        for i, delta in enumerate(moved):
            sideways(delta, True, slot + i).wait_send()
        slot += len(moved)
    pre_own.wait()
    for shift in range(1, row_size):
        pre_copies[shift - 1].wait_send()
        source = lax.rem(row + row_size - shift, row_size)
        pltpu.make_async_remote_copy(
            src_ref=pre_ref, dst_ref=pre_full_ref.at[source],
            send_sem=pre_send.at[shift - 1], recv_sem=pre_recv.at[shift - 1],
            device_id={"row": lax.rem(row + shift, row_size)}, device_id_type=MESH,
        ).wait_recv()
    for copy in out_copies:
        copy.wait()


def gather_and_multiply(row_size, col_size, out_grad, preact, weight):
    chips, half = col_size // 2, col_size // 4
    block, width = out_grad.shape
    tokens, hidden = block * col_size, weight.shape[0]
    dma = pltpu.SemaphoreType.DMA
    anywhere = pl.BlockSpec(memory_space=pl.ANY)
    vmem = pl.BlockSpec(memory_space=pltpu.VMEM)
    flops = 2 * tokens * hidden * width
    return pl.pallas_call(
        functools.partial(gather_kernel, row_size, chips),
        out_shape=(
            jax.ShapeDtypeStruct((col_size, block, width), jnp.bfloat16),
            jax.ShapeDtypeStruct((row_size,) + preact.shape, jnp.bfloat16),
            jax.ShapeDtypeStruct((tokens, hidden), jnp.float32),
            jax.ShapeDtypeStruct((tokens, hidden), jnp.bfloat16),
        ),
        in_specs=[anywhere] * 3,
        out_specs=(vmem, anywhere, anywhere, anywhere),
        scratch_shapes=[
            pltpu.VMEM(weight.shape, jnp.bfloat16),
            pltpu.VMEM((4 * block, width), jnp.bfloat16),
            pltpu.VMEM((tokens, hidden), jnp.float32),
            pltpu.VMEM((tokens, hidden), jnp.bfloat16),
            dma((hidden // tile_of(hidden),)), dma((2,)), dma((chips,)), dma((chips,)),
            dma((max(row_size - 1, 1),)), dma((max(row_size - 1, 1),)),
            dma((half,)), dma((half,)), dma((half,)), dma((half,)), dma((2,)),
        ],
        compiler_params=pltpu.CompilerParams(
            collective_id=0, has_side_effects=True, vmem_limit_bytes=VMEM_LIMIT
        ),
        cost_estimate=pl.CostEstimate(flops=4 * flops, bytes_accessed=30 << 20, transcendentals=0),
        name="gather_grad",
    )(out_grad, preact, weight)


def scatter_kernel(
    chips, pre_ref, weight_ref, out_ref,
    weight, rows, kept, side_out, side_in, right_out, right_in, left_out, left_in,
    weight_sem, side_send, side_recv, right_send, right_recv, left_send, left_recv,
):
    col = lax.axis_index("col")
    chip, core = lax.div(col, 2), lax.rem(col, 2)
    place = ring_position(chip, chips)
    at = lambda delta: 2 * ring_chip(place + delta, chips) + core
    right, left, side = at(1), at(-1), 2 * chip + 1 - core
    half = chips // 2
    width = weight.shape[0]
    cut = cut_of(width)
    tile = tile_of(width)
    tiles = width // tile
    block = out_ref.shape[0]

    for j in range(tiles):
        piece = pl.ds(j * tile, tile)
        pltpu.make_async_copy(weight_ref.at[piece], weight.at[piece], weight_sem.at[j]).start()
    enter((right, left, side), 1, 0)

    def remote(src, dst, peer, send, recv):
        return pltpu.make_async_remote_copy(
            src_ref=src, dst_ref=dst, send_sem=send, recv_sem=recv,
            device_id={"col": peer}, device_id_type=MESH,
        )

    def sideways(group, count):
        piece = pl.ds(0, count)
        return remote(
            side_out.at[group, piece], side_in.at[group, piece], side,
            side_send.at[group], side_recv.at[group],
        )

    def multiply(deltas, group):
        count = block * len(deltas)
        for i, delta in enumerate(deltas):
            mine = at(delta)
            other = mine + 1 - 2 * core
            rows[pl.ds(block * i, block), :] = pre_ref[
                pl.ds(pl.multiple_of(other * block, block), block), :]
            rows[pl.ds(count + block * i, block), :] = pre_ref[
                pl.ds(pl.multiple_of(mine * block, block), block), :]

        @pl.loop(0, tiles)
        def _(j):
            piece = pl.ds(pl.multiple_of(j * tile, tile), tile)
            if group == 0:
                pltpu.make_async_copy(
                    weight_ref.at[piece], weight.at[piece], weight_sem.at[j]
                ).wait()
            part = contract_cols(rows[pl.ds(0, 2 * count), :], weight[piece, :])
            side_out[group, pl.ds(0, count), piece] = part[:count].astype(jnp.bfloat16)
            kept[group, pl.ds(0, count), piece] = part[count:]

        sideways(group, count).start()
        sideways(group, count).wait_recv()

    def total(group, i, lo, size):
        piece, cols = pl.ds(block * i, block), pl.ds(lo, size)
        return kept[group, piece, cols] + side_in[group, piece, cols].astype(jnp.float32)

    def go_right(step):
        size = cut if step == 1 else width
        return remote(
            right_out.at[step - 1, :, pl.ds(0, size)], right_in.at[step - 1, :, pl.ds(0, size)],
            right, right_send.at[step - 1], right_recv.at[step - 1],
        )

    def go_left(step):
        lo, size = (cut, width - cut) if step == 1 else (0, width)
        return remote(
            left_out.at[step - 1, :, pl.ds(lo, size)], left_in.at[step - 1, :, pl.ds(lo, size)],
            left, left_send.at[step - 1], left_recv.at[step - 1],
        )

    def arrived(ref, step, lo, size):
        return ref[step - 2, :, pl.ds(lo, size)].astype(jnp.float32)

    low = lambda value: value.astype(jnp.bfloat16)
    rest = width - cut
    multiply((half,), 0)
    right_out[0, :, pl.ds(0, cut)] = low(total(0, 0, 0, cut))
    go_right(1).start()
    left_out[0, :, pl.ds(cut, rest)] = low(total(0, 0, cut, rest))
    go_left(1).start()
    for step in range(2, half + 1):
        delta = half - step + 1
        group = step - 1
        multiply((delta, -delta), group)
        go_right(step - 1).wait_recv()
        if step == 2:
            right_out[1, :, pl.ds(0, cut)] = low(
                total(1, 0, 0, cut) + arrived(right_in, 2, 0, cut))
            right_out[1, :, pl.ds(cut, rest)] = low(total(1, 0, cut, rest))
        else:
            right_out[group, :, :] = low(
                total(group, 0, 0, width) + arrived(right_in, step, 0, width))
        go_right(step).start()
        go_left(step - 1).wait_recv()
        if step == 2:
            left_out[1, :, pl.ds(0, cut)] = low(total(1, 1, 0, cut))
            left_out[1, :, pl.ds(cut, rest)] = low(
                total(1, 1, cut, rest) + arrived(left_in, 2, cut, rest))
        else:
            left_out[group, :, :] = low(
                total(group, 1, 0, width) + arrived(left_in, step, 0, width))
        go_left(step).start()
    multiply((0,), half)
    go_right(half).wait_recv()
    go_left(half).wait_recv()
    out_ref[...] = (
        total(half, 0, 0, width)
        + arrived(right_in, half + 1, 0, width)
        + arrived(left_in, half + 1, 0, width)
    )
    for step in range(1, half + 1):
        go_right(step).wait_send()
        go_left(step).wait_send()
    for group in range(half + 1):
        sideways(group, block if group in (0, half) else 2 * block).wait_send()


def multiply_and_scatter(col_size, grad_pre, weight):
    chips, half = col_size // 2, col_size // 4
    tokens, hidden = grad_pre.shape
    width = weight.shape[0]
    block = tokens // col_size
    dma = pltpu.SemaphoreType.DMA
    anywhere = pl.BlockSpec(memory_space=pl.ANY)
    vmem = pl.BlockSpec(memory_space=pltpu.VMEM)
    low, ring, group = jnp.bfloat16, (half, block, width), (half + 1, 2 * block, width)
    return pl.pallas_call(
        functools.partial(scatter_kernel, chips),
        out_shape=jax.ShapeDtypeStruct((block, width), jnp.float32),
        in_specs=[vmem, anywhere],
        out_specs=vmem,
        scratch_shapes=[
            pltpu.VMEM(weight.shape, low),
            pltpu.VMEM((4 * block, hidden), low),
            pltpu.VMEM(group, jnp.float32), pltpu.VMEM(group, low), pltpu.VMEM(group, low),
            pltpu.VMEM(ring, low), pltpu.VMEM(ring, low),
            pltpu.VMEM(ring, low), pltpu.VMEM(ring, low),
            dma((width // tile_of(width),)), dma((half + 1,)), dma((half + 1,)),
            dma((half,)), dma((half,)), dma((half,)), dma((half,)),
        ],
        compiler_params=pltpu.CompilerParams(
            collective_id=1, has_side_effects=True, vmem_limit_bytes=VMEM_LIMIT
        ),
        cost_estimate=pl.CostEstimate(
            flops=8 * tokens * hidden * width, bytes_accessed=30 << 20, transcendentals=0
        ),
        name="scatter_sums",
    )(grad_pre, weight)


def outer_kernel(factor, left_ref, right_ref, out_ref):
    out_ref[...] = (contract_rows(left_ref[...], right_ref[...]) * factor).astype(out_ref.dtype)


def scaled_outer(left, right, factor):
    tokens, width = left.shape
    hidden = right.shape[1]
    tile = tile_of(width)
    return pl.pallas_call(
        functools.partial(outer_kernel, factor),
        out_shape=jax.ShapeDtypeStruct((width, hidden), jnp.bfloat16),
        grid=(width // tile,),
        in_specs=[
            pl.BlockSpec((tokens, tile), lambda i: (0, i)),
            pl.BlockSpec((tokens, hidden), lambda i: (0, 0)),
        ],
        out_specs=pl.BlockSpec((tile, hidden), lambda i: (i, 0)),
        compiler_params=pltpu.CompilerParams(vmem_limit_bytes=40 * 1024 * 1024),
        cost_estimate=pl.CostEstimate(
            flops=2 * tokens * hidden * width, bytes_accessed=30 << 20, transcendentals=0
        ),
        name="scaled_outer",
    )(left, right)


def on_device(row_size, col_size, inputs, out_grad, preact, first_weight, second_weight):
    grad_blocks, pre_blocks, partial, partial_low = gather_and_multiply(
        row_size, col_size, out_grad, preact, second_weight
    )
    grad_whole = grad_blocks.reshape(-1, grad_blocks.shape[-1])
    pre_whole = pre_blocks.reshape(-1, pre_blocks.shape[-1]).astype(jnp.float32)
    tokens_all = grad_whole.shape[0]
    factor = 1.0 / math.sqrt(tokens_all)
    inputs, partial_low = lax.optimization_barrier((inputs, partial_low))
    input_whole = lax.all_gather(inputs, "col", axis=0, tiled=True)
    grad_act = partial
    for shift in range(1, row_size):
        turn = [(i, (i + shift) % row_size) for i in range(row_size)]
        grad_act = grad_act + lax.ppermute(partial_low, "row", turn).astype(jnp.float32)
    activated = gelu_value(pre_whole).astype(jnp.bfloat16)
    grad_second = (contract_rows(activated, grad_whole) * factor).astype(jnp.bfloat16)
    grad_pre = (grad_act * gelu_slope(pre_whole)).astype(jnp.bfloat16)
    grad_inputs = multiply_and_scatter(col_size, grad_pre, first_weight)
    grad_first = scaled_outer(input_whole, grad_pre, factor)
    return (grad_inputs, grad_first, grad_second)


def solution(mesh):
    placed = (P("col", "row"), P("col", "row"), P("row", "col"), P("row", "col"), P("col", "row"))
    return jax.shard_map(
        functools.partial(on_device, mesh.shape["row"], mesh.shape["col"]),
        mesh=mesh,
        in_specs=placed,
        out_specs=(P("col", "row"), P("row", "col"), P("col", "row")),
        check_vma=False,
    )
```

```python
import functools
import math

import jax
import jax.numpy as jnp
from jax import lax
from jax.experimental import pallas as pl
from jax.experimental.pallas import tpu as pltpu
from jax.sharding import PartitionSpec as P

INV_ROOT_TWO = 0.7071067811865476
INV_ROOT_TWO_PI = 0.3989422804014327
MESH = pl.DeviceIdType.MESH
VMEM_LIMIT = 58 * 1024 * 1024


def gelu_value(values):
    return 0.5 * values * (1.0 + lax.erf(values * INV_ROOT_TWO))


def gelu_slope(values):
    normal_cdf = 0.5 * (1.0 + lax.erf(values * INV_ROOT_TWO))
    density = jnp.exp(-0.5 * values * values) * INV_ROOT_TWO_PI
    return normal_cdf + values * density


def contract_rows(left, right):
    return lax.dot_general(
        left, right, (((0,), (0,)), ((), ())), preferred_element_type=jnp.float32
    )


def contract_cols(left, right):
    return lax.dot_general(
        left, right, (((1,), (1,)), ((), ())), preferred_element_type=jnp.float32
    )


def tile_of(size):
    return next(t for t in (256, 384, 128, size) if size % t == 0)


def cut_of(width):
    return width // 256 * 128


def ring_position(chip, chips):
    odd = lax.rem(chip, 2)
    half = lax.div(chip, 2)
    return half + odd * (chips - 1 - 2 * half)


def ring_chip(position, chips):
    evens = (chips + 1) // 2
    position = lax.rem(position + 2 * chips, chips)
    upper = (position >= evens).astype(jnp.int32)
    return 2 * position + upper * (2 * (chips - 1 - position) + 1 - 2 * position)


def enter(col_peers, row_size, row):
    barrier = pltpu.get_barrier_semaphore()
    for peer in col_peers:
        pl.semaphore_signal(barrier, inc=1, device_id={"col": peer}, device_id_type=MESH)
    for shift in range(1, row_size):
        pl.semaphore_signal(
            barrier, inc=1, device_id={"row": lax.rem(row + shift, row_size)}, device_id_type=MESH
        )
    pl.semaphore_wait(barrier, len(col_peers) + row_size - 1)


def gather_kernel(
    row_size, chips, grad_ref, pre_ref, weight_ref,
    full_ref, pre_full_ref, sum_ref, low_ref,
    weight, rows, out_sum, out_low,
    weight_sem, local_sem, side_send, side_recv, pre_send, pre_recv,
    right_send, right_recv, left_send, left_recv, store_sem,
):
    row, col = lax.axis_index("row"), lax.axis_index("col")
    chip, core = lax.div(col, 2), lax.rem(col, 2)
    place = ring_position(chip, chips)
    at = lambda delta: 2 * ring_chip(place + delta, chips) + core
    right, left, side = at(1), at(-1), 2 * chip + 1 - core
    half = chips // 2
    tile = tile_of(weight.shape[0])
    tiles = weight.shape[0] // tile
    block = grad_ref.shape[0]
    width = grad_ref.shape[1]
    cut = cut_of(width)

    def weight_copy(j):
        piece = pl.ds(j * tile, tile)
        return pltpu.make_async_copy(weight_ref.at[piece], weight.at[piece], weight_sem.at[j])

    own = pltpu.make_async_copy(grad_ref, full_ref.at[col], local_sem.at[0])
    own.start()
    for j in range(tiles):
        weight_copy(j).start()
    pre_own = pltpu.make_async_copy(pre_ref, pre_full_ref.at[row], local_sem.at[1])
    pre_own.start()
    enter((right, left, side), row_size, row)
    own.wait()

    def to_col(index, lo, size, peer, send, recv):
        piece = full_ref.at[index, :, pl.ds(lo, size)]
        return pltpu.make_async_remote_copy(
            src_ref=piece, dst_ref=piece, send_sem=send, recv_sem=recv,
            device_id={"col": peer}, device_id_type=MESH,
        )

    def go_right(step):
        size = cut if step == half else width
        return to_col(at(1 - step), 0, size, right, right_send.at[step - 1], right_recv.at[step - 1])

    def go_left(step):
        lo, size = (cut, width - cut) if step == half else (0, width)
        return to_col(at(step - 1), lo, size, left, left_send.at[step - 1], left_recv.at[step - 1])

    def from_left(step):
        size = cut if step == half else width
        return to_col(at(-step), 0, size, right, right_send.at[step - 1], right_recv.at[step - 1])

    def from_right(step):
        lo, size = (cut, width - cut) if step == half else (0, width)
        return to_col(at(step), lo, size, left, left_send.at[step - 1], left_recv.at[step - 1])

    def sideways(delta, mine, slot):
        index = at(delta)
        if not mine:
            index = index + 1 - 2 * core
        return to_col(index, 0, width, side, side_send.at[slot], side_recv.at[slot])

    go_right(1).start()
    go_left(1).start()
    sideways(0, True, 0).start()
    pre_copies = []
    for shift in range(1, row_size):
        pre_copies.append(pltpu.make_async_remote_copy(
            src_ref=pre_ref, dst_ref=pre_full_ref.at[row],
            send_sem=pre_send.at[shift - 1], recv_sem=pre_recv.at[shift - 1],
            device_id={"row": lax.rem(row + shift, row_size)}, device_id_type=MESH,
        ))
        pre_copies[-1].start()

    def collect(deltas):
        for i, delta in enumerate(deltas):
            origin = 2 * ring_chip(place + delta, chips)
            for k in range(2):
                rows[pl.ds((2 * i + k) * block, block), :] = full_ref[origin + k]

    def multiply(deltas, first, begin, end):
        count = 2 * block * len(deltas)

        @pl.loop(begin, end)
        def _(j):
            piece = pl.ds(pl.multiple_of(j * tile, tile), tile)
            if first:
                pltpu.make_async_copy(
                    weight_ref.at[piece], weight.at[piece], weight_sem.at[j]
                ).wait()
            part = contract_cols(rows[pl.ds(0, count), :], weight[piece, :])
            low = part.astype(jnp.bfloat16)
            for i, delta in enumerate(deltas):
                origin = pl.multiple_of(2 * block * ring_chip(place + delta, chips), 2 * block)
                out_sum[pl.ds(origin, 2 * block), piece] = part[2 * block * i:2 * block * (i + 1)]
                out_low[pl.ds(origin, 2 * block), piece] = low[2 * block * i:2 * block * (i + 1)]

    slot = 1
    early = tuple(range(2 - half, half - 1))
    late = tuple(d for d in range(1 - half, half + 1) if d not in early)
    sideways(0, False, 0).wait_recv()
    for step in range(1, half + 1):
        if step == half - 1:
            collect(early)
            multiply(early, True, 0, tiles // 2)
        if step == half:
            multiply(early, True, tiles // 2, tiles)
        from_left(step).wait_recv()
        if step < half:
            go_right(step + 1).start()
        from_right(step).wait_recv()
        if step < half:
            go_left(step + 1).start()
        moved = (half,) if step == half else (step, -step)
        for i, delta in enumerate(moved):
            sideways(delta, True, slot + i).start()
        for i, delta in enumerate(moved):
            sideways(delta, False, slot + i).wait_recv()
        slot += len(moved)
    collect(late)
    multiply(late, False, 0, tiles)

    out_copies = [
        pltpu.make_async_copy(out_sum, sum_ref, store_sem.at[0]),
        pltpu.make_async_copy(out_low, low_ref, store_sem.at[1]),
    ]
    for copy in out_copies:
        copy.start()
    for step in range(1, half + 1):
        go_right(step).wait_send()
        go_left(step).wait_send()
    slot = 0
    for step in range(0, half + 1):
        moved = (step,) if step in (0, half) else (step, -step)
        for i, delta in enumerate(moved):
            sideways(delta, True, slot + i).wait_send()
        slot += len(moved)
    pre_own.wait()
    for shift in range(1, row_size):
        pre_copies[shift - 1].wait_send()
        source = lax.rem(row + row_size - shift, row_size)
        pltpu.make_async_remote_copy(
            src_ref=pre_ref, dst_ref=pre_full_ref.at[source],
            send_sem=pre_send.at[shift - 1], recv_sem=pre_recv.at[shift - 1],
            device_id={"row": lax.rem(row + shift, row_size)}, device_id_type=MESH,
        ).wait_recv()
    for copy in out_copies:
        copy.wait()


def gather_and_multiply(row_size, col_size, out_grad, preact, weight):
    chips, half = col_size // 2, col_size // 4
    block, width = out_grad.shape
    tokens, hidden = block * col_size, weight.shape[0]
    dma = pltpu.SemaphoreType.DMA
    anywhere = pl.BlockSpec(memory_space=pl.ANY)
    vmem = pl.BlockSpec(memory_space=pltpu.VMEM)
    flops = 2 * tokens * hidden * width
    return pl.pallas_call(
        functools.partial(gather_kernel, row_size, chips),
        out_shape=(
            jax.ShapeDtypeStruct((col_size, block, width), jnp.bfloat16),
            jax.ShapeDtypeStruct((row_size,) + preact.shape, jnp.bfloat16),
            jax.ShapeDtypeStruct((tokens, hidden), jnp.float32),
            jax.ShapeDtypeStruct((tokens, hidden), jnp.bfloat16),
        ),
        in_specs=[anywhere] * 3,
        out_specs=(vmem, anywhere, anywhere, anywhere),
        scratch_shapes=[
            pltpu.VMEM(weight.shape, jnp.bfloat16),
            pltpu.VMEM((tokens, width), jnp.bfloat16),
            pltpu.VMEM((tokens, hidden), jnp.float32),
            pltpu.VMEM((tokens, hidden), jnp.bfloat16),
            dma((hidden // tile_of(hidden),)), dma((2,)), dma((chips,)), dma((chips,)),
            dma((max(row_size - 1, 1),)), dma((max(row_size - 1, 1),)),
            dma((half,)), dma((half,)), dma((half,)), dma((half,)), dma((2,)),
        ],
        compiler_params=pltpu.CompilerParams(
            collective_id=0, has_side_effects=True, vmem_limit_bytes=VMEM_LIMIT
        ),
        cost_estimate=pl.CostEstimate(flops=4 * flops, bytes_accessed=30 << 20, transcendentals=0),
        name="gather_grad",
    )(out_grad, preact, weight)


def scatter_kernel(
    chips, pre_ref, weight_ref, out_ref,
    weight, rows, kept, side_out, side_in, right_out, right_in, left_out, left_in,
    weight_sem, side_send, side_recv, right_send, right_recv, left_send, left_recv,
):
    col = lax.axis_index("col")
    chip, core = lax.div(col, 2), lax.rem(col, 2)
    place = ring_position(chip, chips)
    at = lambda delta: 2 * ring_chip(place + delta, chips) + core
    right, left, side = at(1), at(-1), 2 * chip + 1 - core
    half = chips // 2
    width = weight.shape[0]
    cut = cut_of(width)
    tile = tile_of(width)
    tiles = width // tile
    block = out_ref.shape[0]

    for j in range(tiles):
        piece = pl.ds(j * tile, tile)
        pltpu.make_async_copy(weight_ref.at[piece], weight.at[piece], weight_sem.at[j]).start()
    enter((right, left, side), 1, 0)

    def remote(src, dst, peer, send, recv):
        return pltpu.make_async_remote_copy(
            src_ref=src, dst_ref=dst, send_sem=send, recv_sem=recv,
            device_id={"col": peer}, device_id_type=MESH,
        )

    def sideways(group, count):
        piece = pl.ds(0, count)
        return remote(
            side_out.at[group, piece], side_in.at[group, piece], side,
            side_send.at[group], side_recv.at[group],
        )

    def members(group):
        delta = half - group
        return (delta,) if group in (0, half) else (delta, -delta)

    def collect(groups):
        start = 0
        for flip in (1, 0):
            for group in groups:
                for delta in members(group):
                    source = at(delta) + flip * (1 - 2 * core)
                    rows[pl.ds(start, block), :] = pre_ref[
                        pl.ds(pl.multiple_of(source * block, block), block), :]
                    start += block

    def multiply(groups, first, begin, end):
        counts = [block * len(members(group)) for group in groups]
        count = sum(counts)

        @pl.loop(begin, end)
        def _(j):
            piece = pl.ds(pl.multiple_of(j * tile, tile), tile)
            if first:
                pltpu.make_async_copy(
                    weight_ref.at[piece], weight.at[piece], weight_sem.at[j]
                ).wait()
            part = contract_cols(rows[pl.ds(0, 2 * count), :], weight[piece, :])
            start = 0
            for group, size in zip(groups, counts):
                side_out[group, pl.ds(0, size), piece] = part[start:start + size].astype(
                    jnp.bfloat16)
                kept[group, pl.ds(0, size), piece] = part[count + start:count + start + size]
                start += size

    def exchange(groups):
        sizes = [block * len(members(group)) for group in groups]
        for group, size in zip(groups, sizes):
            sideways(group, size).start()
        for group, size in zip(groups, sizes):
            sideways(group, size).wait_recv()

    def total(group, i, lo, size):
        piece, cols = pl.ds(block * i, block), pl.ds(lo, size)
        return kept[group, piece, cols] + side_in[group, piece, cols].astype(jnp.float32)

    def go_right(step):
        size = cut if step == 1 else width
        return remote(
            right_out.at[step - 1, :, pl.ds(0, size)], right_in.at[step - 1, :, pl.ds(0, size)],
            right, right_send.at[step - 1], right_recv.at[step - 1],
        )

    def go_left(step):
        lo, size = (cut, width - cut) if step == 1 else (0, width)
        return remote(
            left_out.at[step - 1, :, pl.ds(lo, size)], left_in.at[step - 1, :, pl.ds(lo, size)],
            left, left_send.at[step - 1], left_recv.at[step - 1],
        )

    def arrived(ref, step, lo, size):
        return ref[step - 2, :, pl.ds(lo, size)].astype(jnp.float32)

    low = lambda value: value.astype(jnp.bfloat16)
    rest = width - cut
    early, late = tuple(range(0, 2)), tuple(range(2, half + 1))
    collect(early)
    multiply(early, True, 0, tiles)
    exchange(early)
    right_out[0, :, pl.ds(0, cut)] = low(total(0, 0, 0, cut))
    go_right(1).start()
    left_out[0, :, pl.ds(cut, rest)] = low(total(0, 0, cut, rest))
    go_left(1).start()
    for step in range(2, half + 1):
        group = step - 1
        if step == 2:
            collect(late)
            multiply(late, False, 0, tiles // 2)
        if step == 3:
            multiply(late, False, tiles // 2, tiles)
            exchange(late)
        go_right(step - 1).wait_recv()
        if step == 2:
            right_out[1, :, pl.ds(0, cut)] = low(
                total(1, 0, 0, cut) + arrived(right_in, 2, 0, cut))
            right_out[1, :, pl.ds(cut, rest)] = low(total(1, 0, cut, rest))
        else:
            right_out[group, :, :] = low(
                total(group, 0, 0, width) + arrived(right_in, step, 0, width))
        go_right(step).start()
        go_left(step - 1).wait_recv()
        if step == 2:
            left_out[1, :, pl.ds(0, cut)] = low(total(1, 1, 0, cut))
            left_out[1, :, pl.ds(cut, rest)] = low(
                total(1, 1, cut, rest) + arrived(left_in, 2, cut, rest))
        else:
            left_out[group, :, :] = low(
                total(group, 1, 0, width) + arrived(left_in, step, 0, width))
        go_left(step).start()
    go_right(half).wait_recv()
    go_left(half).wait_recv()
    out_ref[...] = (
        total(half, 0, 0, width)
        + arrived(right_in, half + 1, 0, width)
        + arrived(left_in, half + 1, 0, width)
    )
    for step in range(1, half + 1):
        go_right(step).wait_send()
        go_left(step).wait_send()
    for group in range(half + 1):
        sideways(group, block if group in (0, half) else 2 * block).wait_send()


def multiply_and_scatter(col_size, grad_pre, weight):
    chips, half = col_size // 2, col_size // 4
    tokens, hidden = grad_pre.shape
    width = weight.shape[0]
    block = tokens // col_size
    dma = pltpu.SemaphoreType.DMA
    anywhere = pl.BlockSpec(memory_space=pl.ANY)
    vmem = pl.BlockSpec(memory_space=pltpu.VMEM)
    low, ring, group = jnp.bfloat16, (half, block, width), (half + 1, 2 * block, width)
    return pl.pallas_call(
        functools.partial(scatter_kernel, chips),
        out_shape=jax.ShapeDtypeStruct((block, width), jnp.float32),
        in_specs=[vmem, anywhere],
        out_specs=vmem,
        scratch_shapes=[
            pltpu.VMEM(weight.shape, low),
            pltpu.VMEM((tokens, hidden), low),
            pltpu.VMEM(group, jnp.float32), pltpu.VMEM(group, low), pltpu.VMEM(group, low),
            pltpu.VMEM(ring, low), pltpu.VMEM(ring, low),
            pltpu.VMEM(ring, low), pltpu.VMEM(ring, low),
            dma((width // tile_of(width),)), dma((half + 1,)), dma((half + 1,)),
            dma((half,)), dma((half,)), dma((half,)), dma((half,)),
        ],
        compiler_params=pltpu.CompilerParams(
            collective_id=1, has_side_effects=True, vmem_limit_bytes=VMEM_LIMIT
        ),
        cost_estimate=pl.CostEstimate(
            flops=8 * tokens * hidden * width, bytes_accessed=30 << 20, transcendentals=0
        ),
        name="scatter_sums",
    )(grad_pre, weight)


def outer_kernel(factor, left_ref, right_ref, out_ref):
    out_ref[...] = (contract_rows(left_ref[...], right_ref[...]) * factor).astype(out_ref.dtype)


def scaled_outer(left, right, factor):
    tokens, width = left.shape
    hidden = right.shape[1]
    tile = tile_of(width)
    return pl.pallas_call(
        functools.partial(outer_kernel, factor),
        out_shape=jax.ShapeDtypeStruct((width, hidden), jnp.bfloat16),
        grid=(width // tile,),
        in_specs=[
            pl.BlockSpec((tokens, tile), lambda i: (0, i)),
            pl.BlockSpec((tokens, hidden), lambda i: (0, 0)),
        ],
        out_specs=pl.BlockSpec((tile, hidden), lambda i: (i, 0)),
        compiler_params=pltpu.CompilerParams(vmem_limit_bytes=40 * 1024 * 1024),
        cost_estimate=pl.CostEstimate(
            flops=2 * tokens * hidden * width, bytes_accessed=30 << 20, transcendentals=0
        ),
        name="scaled_outer",
    )(left, right)


def on_device(row_size, col_size, inputs, out_grad, preact, first_weight, second_weight):
    grad_blocks, pre_blocks, partial, partial_low = gather_and_multiply(
        row_size, col_size, out_grad, preact, second_weight
    )
    grad_whole = grad_blocks.reshape(-1, grad_blocks.shape[-1])
    pre_whole = pre_blocks.reshape(-1, pre_blocks.shape[-1]).astype(jnp.float32)
    tokens_all = grad_whole.shape[0]
    factor = 1.0 / math.sqrt(tokens_all)
    inputs, partial_low = lax.optimization_barrier((inputs, partial_low))
    input_whole = lax.all_gather(inputs, "col", axis=0, tiled=True)
    grad_act = partial
    for shift in range(1, row_size):
        turn = [(i, (i + shift) % row_size) for i in range(row_size)]
        grad_act = grad_act + lax.ppermute(partial_low, "row", turn).astype(jnp.float32)
    activated = gelu_value(pre_whole).astype(jnp.bfloat16)
    grad_second = (contract_rows(activated, grad_whole) * factor).astype(jnp.bfloat16)
    grad_pre = (grad_act * gelu_slope(pre_whole)).astype(jnp.bfloat16)
    grad_inputs = multiply_and_scatter(col_size, grad_pre, first_weight)
    grad_first = scaled_outer(input_whole, grad_pre, factor)
    return (grad_inputs, grad_first, grad_second)


def solution(mesh):
    placed = (P("col", "row"), P("col", "row"), P("row", "col"), P("row", "col"), P("col", "row"))
    return jax.shard_map(
        functools.partial(on_device, mesh.shape["row"], mesh.shape["col"]),
        mesh=mesh,
        in_specs=placed,
        out_specs=(P("col", "row"), P("row", "col"), P("col", "row")),
        check_vma=False,
    )
```
